512 devices in a mesh: ctx: 64 (over y, z_lo, core), ch: 8 (over z_hi, x).
Axes of the slice: x: 4, y: 4, z: 16 (z_hi: 2, z_lo: 8; z = z_hi * 8 + z_lo), core: 2. Of those that a mesh axis runs over, the one named last changes fastest.
Arguments:
- x_one: bfloat16 [8192, 4096], P('ctx', 'ch'), may hold values from -6 to 6
- x_two: bfloat16 [8192, 4096], P('ctx', 'ch'), may hold values from -6 to 6
- values: bfloat16 [8192, 4096], P('ctx', 'ch'), may hold values from -6 to 6
- grad_out: bfloat16 [8192, 4096], P('ctx', 'ch'), may hold values from -3 to 3
- filter_raw: bfloat16 [1024, 512], P('ctx', 'ch'), may hold values from -4 to 4
Outputs:
- grad_x_one: bfloat16 [8192, 4096], P('ctx', 'ch')
- grad_x_two: bfloat16 [8192, 4096], P('ctx', 'ch')
- grad_values: bfloat16 [8192, 4096], P('ctx', 'ch')
- grad_filter: float32 [1024, 512], P('ctx', 'ch')
The draws below stay inside these ranges and needn't reach their ends.
All inputs are finite; a program needn't handle non-finite values.
Results may differ from the reference program's by a relative error of at most 0.0049.
Values may be sent and summed in bfloat16 or wider, within the bound.
A program may use at most 64 MiB of HBM per device.

```python
import math
import jax
import jax.numpy as jnp
from jax import lax

C = 4096
F = 512
L = 1024
TOKENS = 8192


def shard_levels(rng, dims, split, least, largest):
    gain = 1.0
    for axis_at, shards_of in split:
        draws = jax.random.uniform(jax.random.fold_in(jax.random.fold_in(rng, 6), axis_at), (shards_of,), jnp.float32, least / len(split), largest / len(split))
        gain = gain * jnp.repeat(jnp.exp(draws), dims[axis_at] // shards_of).reshape((-1,) + (1,) * (len(dims) - 1 - axis_at))
    return gain


def noise(stream_key, dims, width, reach, shards=(), kind=jnp.bfloat16):
    drawn = jax.random.normal(stream_key, dims, jnp.float32) * width
    if len(shards) > 0:
        drawn = shard_levels(stream_key, dims, shards, -0.22, 0.18) * drawn
    return jnp.clip(drawn, min=-reach, max=reach).astype(kind)


def setup_inputs(seed: int = 0) -> dict:
    splits = jax.random.split(jax.random.key(seed), 6)
    return {
        "x_one": noise(splits[0], (TOKENS, C), 1.0, 6.0, ((0, 64), (1, 8))),
        "x_two": noise(splits[1], (TOKENS, C), 1.0, 6.0, ((0, 64), (1, 8))),
        "values": noise(splits[2], (TOKENS, C), 1.0, 6.0, ((0, 64), (1, 8))),
        "grad_out": noise(splits[3], (TOKENS, C), 0.5, 3.0, ((0, 64), (1, 8))),
        "filter_raw": noise(splits[4], (L, F), 1.0, 4.0, ((0, 64), (1, 8))),
    }


def reference(x_one, x_two, values, grad_out, filter_raw):
    scale = 1.0 / math.sqrt(L)
    length = 2 * TOKENS
    blocks = C // F
    filt = filter_raw.astype(jnp.float32) * scale
    filt_spec = jnp.fft.rfft(filt, length, axis=0)
    product_in = (x_one.astype(jnp.float32) * values.astype(jnp.float32)).astype(jnp.bfloat16)
    grad_conv = (grad_out.astype(jnp.float32) * x_two.astype(jnp.float32)).astype(jnp.bfloat16)

    def arrange(array):
        return array.reshape(TOKENS, blocks, F).transpose(1, 0, 2)

    def per_block(items):
        prod_blk, grad_blk, out_blk, val_blk, one_blk = items
        prod_spec = jnp.fft.rfft(prod_blk.astype(jnp.float32), length, axis=0)
        grad_spec = jnp.fft.rfft(grad_blk.astype(jnp.float32), length, axis=0)
        conv_out = jnp.fft.irfft(prod_spec * filt_spec, length, axis=0)[:TOKENS]
        grad_in = jnp.fft.irfft(jnp.conj(filt_spec) * grad_spec, length, axis=0)[:TOKENS]
        corr = jnp.fft.irfft(jnp.conj(prod_spec) * grad_spec, length, axis=0)[:L]
        first = (grad_in * val_blk.astype(jnp.float32)).astype(jnp.bfloat16)
        second = (out_blk.astype(jnp.float32) * conv_out).astype(jnp.bfloat16)
        third = (grad_in * one_blk.astype(jnp.float32)).astype(jnp.bfloat16)
        return (first, second, third, corr)
    first, second, third, corr = lax.map(per_block, (arrange(product_in), arrange(grad_conv), arrange(grad_out), arrange(values), arrange(x_one)))

    def restore(array):
        return array.transpose(1, 0, 2).reshape(TOKENS, C)
    grad_filter = lax.optimization_barrier(jnp.sum(corr, axis=0)) * scale
    return (restore(first), restore(second), restore(third), grad_filter)
```

```python
import functools
import math

import jax
import jax.numpy as jnp
from jax import lax
from jax.experimental import pallas as pl
from jax.experimental.pallas import tpu as pltpu
from jax.sharding import PartitionSpec as P

MESH = pl.DeviceIdType.MESH
F32 = jnp.float32
BF16 = jnp.bfloat16
LANES = 128
GROUP = 8


def kernel(
    peers,
    slabs,
    scale,
    x_one_ref,
    x_two_ref,
    values_ref,
    grad_out_ref,
    raw_ref,
    d_one_ref,
    d_two_ref,
    d_values_ref,
    d_filter_ref,
    send_in,
    recv_in,
    send_out,
    recv_out,
    spread,
    prod,
    grad,
    conv_full,
    back_full,
    piece,
    gathered,
    filters,
    taps_rows,
    toeplitz,
    terms,
    term_in,
    term_out,
    owned,
    send_sem,
    recv_sem,
):
    me = lax.axis_index("ctx")
    slab = lax.axis_index("ch")
    tok = x_one_ref.shape[0]
    chans = x_one_ref.shape[1]
    share = peers // slabs
    reach = filters.shape[0] // GROUP
    lead = reach
    mine = me // share
    local_piece = lax.rem(me, share)

    barrier = pltpu.get_barrier_semaphore()

    @pl.loop(1, peers)
    def _(step):
        other = lax.rem(me + step, peers)
        pl.semaphore_signal(barrier, inc=1, device_id={"ctx": other}, device_id_type=MESH)

    @pl.loop(1, slabs)
    def _(step):
        other = lax.rem(slab + step, slabs)
        pl.semaphore_signal(barrier, inc=1, device_id={"ch": other}, device_id_type=MESH)

    @pl.loop(0, share)
    def _(q):
        @pl.when(jnp.logical_or(mine != slab, q != local_piece))
        def _():
            pl.semaphore_signal(
                barrier,
                inc=1,
                device_id={"ctx": slab * share + q, "ch": mine},
                device_id_type=MESH,
            )

    raw = raw_ref[...]
    depth = raw.shape[0]
    row = lax.broadcasted_iota(jnp.int32, (depth, LANES), 0)
    col = lax.broadcasted_iota(jnp.int32, (depth, LANES), 1)
    pick = lax.rem(col, depth) == row
    laid = lax.dot_general(
        raw,
        jnp.where(pick, 1.0, 0.0).astype(BF16),
        (((0,), (0,)), ((), ())),
        preferred_element_type=F32,
    )
    at_row = lax.broadcasted_iota(jnp.int32, laid.shape, 0)
    at_col = lax.broadcasted_iota(jnp.int32, laid.shape, 1)
    own_group = lax.rem(at_row, GROUP) == at_col // depth
    laid = jnp.where(own_group, laid, 0.0)
    piece[...] = jnp.sum(laid.reshape(share, GROUP, LANES), axis=1)

    def lay(left, right):
        product = (left[...].astype(F32) * right[...].astype(F32)).T
        return product.astype(BF16).reshape(peers, GROUP, tok)

    send_in[0] = lay(x_one_ref, values_ref)
    send_in[1] = lay(grad_out_ref, x_two_ref)
    pl.semaphore_wait(barrier, peers - 1 + slabs - 1 + share - jnp.where(mine == slab, 1, 0))

    def copy(src, dst, at, target):
        return pltpu.make_async_remote_copy(
            src_ref=src,
            dst_ref=dst,
            send_sem=send_sem.at[at],
            recv_sem=recv_sem.at[at],
            device_id=target,
            device_id_type=MESH,
        )

    @pl.loop(0, share)
    def _(q):
        @pl.when(jnp.logical_or(mine != slab, q != local_piece))
        def _():
            copy(
                piece.at[pl.ds(q, 1)],
                gathered.at[pl.ds(me, 1)],
                0,
                {"ctx": slab * share + q},
            ).start()

    for which in range(2):

        @pl.loop(1, peers)
        def _(step):
            other = lax.rem(me + step, peers)
            copy(
                send_in.at[which, other], recv_in.at[which, me], 1 + which, {"ctx": other}
            ).start()

    for which in range(2):
        recv_in[which, pl.ds(me, 1)] = send_in[which, pl.ds(me, 1)]

    @pl.when(mine == slab)
    def _():
        gathered[pl.ds(me, 1)] = piece[pl.ds(local_piece, 1)]
        rest = gathered.at[pl.ds(0, peers - 1)]
        copy(rest, rest, 0, {"ctx": me}).wait_recv()

        @pl.loop(1, slabs)
        def _(step):
            other = lax.rem(slab + step, slabs)
            copy(gathered, filters, 3, {"ch": other}).start()

        filters[...] = gathered[...]

        @pl.loop(1, slabs)
        def _(step):
            copy(gathered, filters, 3, {"ch": slab}).wait_send()

    @pl.when(mine != slab)
    def _():
        copy(gathered, filters, 3, {"ch": slab}).wait_recv()

    lane_group = lax.broadcasted_iota(jnp.int32, (reach, LANES), 1) // depth
    sources = [filters[pl.ds(i, reach, stride=GROUP), :] for i in range(GROUP)]
    for c in range(GROUP):
        line = jnp.zeros((reach, LANES), F32)
        for i in range(GROUP):
            turned = pltpu.roll(sources[i], ((i - c) * depth) % LANES, 1)
            line = jnp.where(lane_group == i, turned, line)
        taps_rows[c] = line * scale

    lower = lax.broadcasted_iota(jnp.int32, (LANES, LANES), 0)
    upper = lax.broadcasted_iota(jnp.int32, (LANES, LANES), 1)
    after = upper >= lower
    within = upper <= lower
    flip = jnp.where(upper + lower == LANES - 1, 1.0, 0.0).astype(BF16)

    @pl.loop(0, GROUP)
    def _(c):
        before = jnp.zeros((LANES, LANES), F32)
        for k in range(reach + 1):
            if k < reach:
                line = jnp.broadcast_to(taps_rows[c, pl.ds(k, 1), :], (LANES, LANES))
                turned = pltpu.roll(line, 0, 1, stride=1, stride_axis=0)
            else:
                turned = jnp.zeros((LANES, LANES), F32)
            toeplitz[c, k] = jnp.where(after, turned, before).astype(BF16)
            before = turned

    blocks = reach + 1

    def take_in(which, padded, at):
        rest = recv_in.at[which, pl.ds(0, peers - 1)]
        copy(rest, rest, 1 + which, {"ctx": me}).wait_recv()
        spread[...] = recv_in[which].astype(F32)
        for c in range(GROUP):
            padded[c, pl.ds(at, peers), :] = spread[:, c, :]

    def send_back(which):
        send_out[which] = spread[...].astype(BF16)

        @pl.loop(1, peers)
        def _(step):
            other = lax.rem(me + step, peers)
            copy(
                send_out.at[which, other], recv_out.at[which, me], 4 + which, {"ctx": other}
            ).start()

        recv_out[which, pl.ds(me, 1)] = send_out[which, pl.ds(me, 1)]

    prod[:, pl.ds(0, lead), :] = jnp.zeros((GROUP, lead, LANES), F32)
    grad[:, pl.ds(peers, lead), :] = jnp.zeros((GROUP, lead, LANES), F32)

    take_in(0, prod, lead)

    @pl.loop(0, GROUP)
    def _(c):
        wide = jnp.concatenate(
            [prod[c, pl.ds(lead - k, peers), :].astype(BF16) for k in range(blocks)], axis=1
        )
        tall = jnp.concatenate([toeplitz[c, k] for k in range(blocks)], axis=0)
        conv_full[c] = jnp.dot(wide, tall, preferred_element_type=F32)

    for c in range(GROUP):
        spread[:, c, :] = conv_full[c]
    send_back(0)

    take_in(1, grad, 0)

    @pl.loop(0, GROUP)
    def _(c):
        wide = jnp.concatenate(
            [grad[c, pl.ds(k, peers), :].astype(BF16) for k in range(blocks)], axis=1
        )
        flat = jnp.concatenate([toeplitz[c, k] for k in range(blocks)], axis=1)
        back_full[c] = lax.dot_general(
            wide, flat, (((1,), (1,)), ((), ())), preferred_element_type=F32
        )

    for c in range(GROUP):
        spread[:, c, :] = back_full[c]
    send_back(1)

    @pl.loop(0, GROUP)
    def _(c):
        wide = jnp.concatenate(
            [grad[c, pl.ds(k, peers), :].astype(BF16) for k in range(blocks)], axis=1
        )
        own = prod[c, pl.ds(lead, peers), :].astype(BF16)
        turned_own = lax.dot_general(
            flip, own, (((1,), (1,)), ((), ())), preferred_element_type=F32
        ).astype(BF16)
        cross = jnp.dot(turned_own, wide, preferred_element_type=F32)
        turned = [
            pltpu.roll(cross[:, k * LANES : (k + 1) * LANES], 1, 1, stride=1, stride_axis=0)
            for k in range(blocks)
        ]
        for k in range(reach):
            both = jnp.where(within, turned[k], turned[k + 1])
            terms[k, pl.ds(c, 1), :] = jnp.sum(both, axis=0, keepdims=True)

    @pl.loop(1, slabs)
    def _(step):
        other = lax.rem(slab + step, slabs)
        copy(terms.at[other], term_in.at[slab], 6, {"ch": other}).start()

    term_in[pl.ds(slab, 1)] = terms[pl.ds(slab, 1)]
    rest = term_in.at[pl.ds(0, slabs - 1)]
    copy(rest, rest, 6, {"ch": slab}).wait_recv()
    total = jnp.sum(term_in[...], axis=0) * scale

    at_row = lax.broadcasted_iota(jnp.int32, total.shape, 0)
    at_col = lax.broadcasted_iota(jnp.int32, total.shape, 1) // depth
    crossed = jnp.zeros_like(total)
    for d in range(GROUP):
        moved = total if d == 0 else pltpu.roll(pltpu.roll(total, GROUP - d, 0), d * depth, 1)
        crossed = jnp.where(lax.rem(at_col - at_row + GROUP, GROUP) == d, moved, crossed)
    term_out[...] = crossed

    @pl.loop(0, share)
    def _(q):
        @pl.when(jnp.logical_or(mine != slab, q != local_piece))
        def _():
            copy(
                term_out.at[pl.ds(q, 1)],
                owned.at[pl.ds(local_piece, 1)],
                7,
                {"ctx": slab * share + q, "ch": mine},
            ).start()

    @pl.when(mine == slab)
    def _():
        owned[pl.ds(local_piece, 1)] = term_out[pl.ds(local_piece, 1)]

    def take_out(which):
        rest = recv_out.at[which, pl.ds(0, peers - 1)]
        copy(rest, rest, 4 + which, {"ctx": me}).wait_recv()
        return recv_out[which].astype(F32).reshape(chans, tok).T

    d_two_ref[...] = (take_out(0) * grad_out_ref[...].astype(F32)).astype(BF16)
    back = take_out(1)
    d_one_ref[...] = (back * values_ref[...].astype(F32)).astype(BF16)
    d_values_ref[...] = (back * x_one_ref[...].astype(F32)).astype(BF16)

    @pl.when(mine == slab)
    def _():
        rest = owned.at[pl.ds(0, share - 1)]
        copy(rest, rest, 7, {"ctx": me}).wait()
        rest = gathered.at[pl.ds(0, share - 1)]
        copy(rest, rest, 0, {"ctx": me}).wait_send()

    @pl.when(mine != slab)
    def _():
        copy(owned, owned, 7, {"ctx": me}).wait()
        rest = gathered.at[pl.ds(0, share)]
        copy(rest, rest, 0, {"ctx": me}).wait_send()

    full = jnp.broadcast_to(owned[...][:, None, :], (share, GROUP, LANES))
    full = full.reshape(share * GROUP, LANES)
    full = jnp.where(own_group, full, 0.0)
    d_filter_ref[...] = lax.dot_general(
        jnp.where(pick, 1.0, 0.0),
        full,
        (((1,), (1,)), ((), ())),
        precision=lax.Precision.HIGHEST,
        preferred_element_type=F32,
    )

    for which in range(2):
        rest = send_in.at[which, pl.ds(0, peers - 1)]
        copy(rest, rest, 1 + which, {"ctx": me}).wait_send()
        rest = send_out.at[which, pl.ds(0, peers - 1)]
        copy(rest, rest, 4 + which, {"ctx": me}).wait_send()
    rest = terms.at[pl.ds(0, slabs - 1)]
    copy(rest, rest, 6, {"ch": slab}).wait_send()


def solution(mesh):
    peers = mesh.shape["ctx"]
    slabs = mesh.shape["ch"]

    def local(x_one, x_two, values, grad_out, filter_raw):
        tok, chans = x_one.shape
        depth, owned = filter_raw.shape
        taps = depth * peers
        reach = taps // LANES
        share = peers // slabs
        blocks = reach + 1
        stream = jax.ShapeDtypeStruct((tok, chans), BF16)
        vmem = pl.BlockSpec(memory_space=pltpu.VMEM)
        return pl.pallas_call(
            functools.partial(kernel, peers, slabs, 1.0 / math.sqrt(taps)),
            out_shape=(
                stream,
                stream,
                stream,
                jax.ShapeDtypeStruct((depth, owned), F32),
            ),
            in_specs=[vmem] * 5,
            out_specs=[vmem] * 4,
            scratch_shapes=[
                pltpu.VMEM((2, peers, GROUP, tok), BF16),
                pltpu.VMEM((2, peers, GROUP, tok), BF16),
                pltpu.VMEM((2, peers, GROUP, tok), BF16),
                pltpu.VMEM((2, peers, GROUP, tok), BF16),
                pltpu.VMEM((peers, GROUP, tok), F32),
                pltpu.VMEM((GROUP, peers + reach, tok), F32),
                pltpu.VMEM((GROUP, peers + reach, tok), F32),
                pltpu.VMEM((GROUP, peers, tok), F32),
                pltpu.VMEM((GROUP, peers, tok), F32),
                pltpu.VMEM((share, LANES), F32),
                pltpu.VMEM((peers, LANES), F32),
                pltpu.VMEM((peers, LANES), F32),
                pltpu.VMEM((GROUP, reach, LANES), F32),
                pltpu.VMEM((GROUP, blocks, LANES, LANES), BF16),
                pltpu.VMEM((slabs, GROUP, LANES), F32),
                pltpu.VMEM((slabs, GROUP, LANES), F32),
                pltpu.VMEM((GROUP, LANES), F32),
                pltpu.VMEM((share, LANES), F32),
                pltpu.SemaphoreType.DMA((8,)),
                pltpu.SemaphoreType.DMA((8,)),
            ],
            compiler_params=pltpu.CompilerParams(
                collective_id=0, has_side_effects=True, vmem_limit_bytes=40 * 1024 * 1024
            ),
        )(x_one, x_two, values, grad_out, filter_raw)

    placed = P("ctx", "ch")
    return jax.shard_map(
        local,
        mesh=mesh,
        in_specs=(placed,) * 5,
        out_specs=(placed,) * 4,
        check_vma=False,
    )
```

```python
import functools
import math

import jax
import jax.numpy as jnp
from jax import lax
from jax.experimental import pallas as pl
from jax.experimental.pallas import tpu as pltpu
from jax.sharding import PartitionSpec as P

MESH = pl.DeviceIdType.MESH
F32 = jnp.float32
BF16 = jnp.bfloat16
LANES = 128
GROUP = 8


def kernel(
    peers,
    slabs,
    scale,
    x_one_in,
    x_two_in,
    values_in,
    grad_out_in,
    raw_in,
    d_one_ref,
    d_two_ref,
    d_values_ref,
    d_filter_ref,
    x_one_ref,
    x_two_ref,
    values_ref,
    grad_out_ref,
    raw_ref,
    send_in,
    recv_in,
    send_out,
    recv_out,
    spread,
    prod,
    grad,
    conv_full,
    back_full,
    piece,
    gathered,
    taps_rows,
    toeplitz,
    terms,
    term_out,
    owned,
    load_sem,
    send_sem,
    recv_sem,
):
    me = lax.axis_index("ctx")
    slab = lax.axis_index("ch")
    tok = x_one_ref.shape[0]
    chans = x_one_ref.shape[1]
    share = peers // slabs
    reach = taps_rows.shape[1]
    lead = reach
    blocks = reach + 1
    mine = me // share
    local_piece = lax.rem(me, share)
    at_home = mine == slab

    loads = [
        pltpu.make_async_copy(src, dst, load_sem.at[n])
        for n, (src, dst) in enumerate(
            (
                (x_one_in, x_one_ref),
                (values_in, values_ref),
                (grad_out_in, grad_out_ref),
                (x_two_in, x_two_ref),
                (raw_in, raw_ref),
            )
        )
    ]
    for load in loads:
        load.start()

    barrier = pltpu.get_barrier_semaphore()

    def greet(target):
        pl.semaphore_signal(barrier, inc=1, device_id=target, device_id_type=MESH)

    @pl.loop(0, share * (slabs - 1))
    def _(n):
        other = lax.rem(slab + 1 + n // share, slabs)
        greet({"ctx": slab * share + lax.rem(n, share), "ch": other})

    @pl.when(jnp.logical_not(at_home))
    def _():
        @pl.loop(0, peers)
        def _(n):
            greet({"ctx": lax.rem(me + n, peers), "ch": mine})

    @pl.loop(1, peers)
    def _(step):
        greet({"ctx": lax.rem(me + step, peers)})

    def copy(src, dst, at, target):
        return pltpu.make_async_remote_copy(
            src_ref=src,
            dst_ref=dst,
            send_sem=send_sem.at[at],
            recv_sem=recv_sem.at[at],
            device_id=target,
            device_id_type=MESH,
        )

    def received(ref, count, at):
        rest = ref.at[pl.ds(0, count)]
        copy(rest, rest, at, {"ctx": me}).wait_recv()

    def sent(ref, count, at):
        rest = ref.at[pl.ds(0, count)]
        copy(rest, rest, at, {"ctx": me}).wait_send()

    def by_home(act, ref, at):
        pl.when(at_home)(lambda: act(ref, peers - 1, at))
        pl.when(jnp.logical_not(at_home))(lambda: act(ref, peers, at))

    half = GROUP // 2
    first_half = lax.broadcasted_iota(jnp.int32, (peers, GROUP, tok), 1) < half

    def lay(left, right):
        product = (left[...].astype(F32) * right[...].astype(F32)).T
        return product.reshape(peers, GROUP, tok)

    for load in loads:
        load.wait()
    prods = lay(x_one_ref, values_ref)
    grads = lay(grad_out_ref, x_two_ref)
    send_in[0] = jnp.where(first_half, prods, pltpu.roll(grads, half, 1)).astype(BF16)
    send_in[1] = jnp.where(first_half, pltpu.roll(prods, half, 1), grads).astype(BF16)

    raw = raw_ref[...]
    depth = raw.shape[0]
    row = lax.broadcasted_iota(jnp.int32, (depth, LANES), 0)
    col = lax.broadcasted_iota(jnp.int32, (depth, LANES), 1)
    pick = lax.rem(col, depth) == row
    laid = lax.dot_general(
        raw,
        jnp.where(pick, 1.0, 0.0).astype(BF16),
        (((0,), (0,)), ((), ())),
        preferred_element_type=F32,
    )
    at_row = lax.broadcasted_iota(jnp.int32, laid.shape, 0)
    at_col = lax.broadcasted_iota(jnp.int32, laid.shape, 1)
    own_group = lax.rem(at_row, GROUP) == at_col // depth
    laid = jnp.where(own_group, laid, 0.0)
    piece[...] = jnp.sum(laid.reshape(share, GROUP, LANES), axis=1)

    prod[:, pl.ds(0, lead), :] = jnp.zeros((GROUP, lead, LANES), F32)
    grad[:, pl.ds(peers, lead), :] = jnp.zeros((GROUP, lead, LANES), F32)

    pl.semaphore_wait(
        barrier, peers - 1 + share * (slabs - 1) + jnp.where(at_home, 0, peers)
    )

    def exchange(source, target, part, at):
        @pl.loop(1, peers)
        def _(step):
            other = lax.rem(me + step, peers)
            copy(source.at[part, other], target.at[part, me], at + part, {"ctx": other}).start()

    exchange(send_in, recv_in, 0, 0)

    @pl.loop(0, share * slabs)
    def _(n):
        turn, q = n // share, lax.rem(n, share)
        itself = jnp.logical_and(at_home, jnp.logical_and(turn == 0, q == local_piece))

        @pl.when(jnp.logical_not(itself))
        def _():
            copy(
                piece.at[pl.ds(q, 1)],
                gathered.at[pl.ds(me, 1)],
                4,
                {"ctx": slab * share + q, "ch": lax.rem(slab + turn, slabs)},
            ).start()

    exchange(send_in, recv_in, 1, 0)
    for part in range(2):
        recv_in[part, pl.ds(me, 1)] = send_in[part, pl.ds(me, 1)]

    @pl.when(at_home)
    def _():
        gathered[pl.ds(me, 1)] = piece[pl.ds(local_piece, 1)]

    lower = lax.broadcasted_iota(jnp.int32, (LANES, LANES), 0)
    upper = lax.broadcasted_iota(jnp.int32, (LANES, LANES), 1)
    after = upper >= lower
    within = upper <= lower
    flip = jnp.where(upper + lower == LANES - 1, 1.0, 0.0).astype(BF16)

    def take_in(part):
        received(recv_in.at[part], peers - 1, part)
        spread[...] = recv_in[part].astype(F32)
        for c in range(half):
            prod[part * half + c, pl.ds(lead, peers), :] = spread[:, c, :]
            grad[part * half + c, pl.ds(0, peers), :] = spread[:, half + c, :]

    def correlate(part):
        @pl.loop(part * half, part * half + half)
        def _(c):
            wide = jnp.concatenate(
                [grad[c, pl.ds(k, peers), :].astype(BF16) for k in range(blocks)], axis=1
            )
            own = prod[c, pl.ds(lead, peers), :].astype(BF16)
            turned_own = lax.dot_general(
                flip, own, (((1,), (1,)), ((), ())), preferred_element_type=F32
            ).astype(BF16)
            cross = jnp.dot(turned_own, wide, preferred_element_type=F32)
            turned = [
                pltpu.roll(cross[:, k * LANES : (k + 1) * LANES], 1, 1, stride=1, stride_axis=0)
                for k in range(blocks)
            ]
            for k in range(reach):
                both = jnp.where(within, turned[k], turned[k + 1])
                terms[k, pl.ds(c, 1), :] = jnp.sum(both, axis=0, keepdims=True)

    def convolve(part):
        @pl.loop(part * half, part * half + half)
        def _(c):
            wide = jnp.concatenate(
                [prod[c, pl.ds(lead - k, peers), :].astype(BF16) for k in range(blocks)], axis=1
            )
            tall = jnp.concatenate([toeplitz[c, k] for k in range(blocks)], axis=0)
            conv_full[c] = jnp.dot(wide, tall, preferred_element_type=F32)
            wide = jnp.concatenate(
                [grad[c, pl.ds(k, peers), :].astype(BF16) for k in range(blocks)], axis=1
            )
            flat = jnp.concatenate([toeplitz[c, k] for k in range(blocks)], axis=1)
            back_full[c] = lax.dot_general(
                wide, flat, (((1,), (1,)), ((), ())), preferred_element_type=F32
            )

        for c in range(half):
            spread[:, c, :] = conv_full[part * half + c]
            spread[:, half + c, :] = back_full[part * half + c]
        send_out[part] = spread[...].astype(BF16)
        exchange(send_out, recv_out, part, 2)
        recv_out[part, pl.ds(me, 1)] = send_out[part, pl.ds(me, 1)]

    take_in(0)
    correlate(0)

    by_home(received, gathered, 4)
    lane_group = lax.broadcasted_iota(jnp.int32, (reach, LANES), 1) // depth
    sources = [gathered[pl.ds(i, reach, stride=GROUP), :] for i in range(GROUP)]
    for c in range(GROUP):
        line = jnp.zeros((reach, LANES), F32)
        for i in range(GROUP):
            turned = pltpu.roll(sources[i], ((i - c) * depth) % LANES, 1)
            line = jnp.where(lane_group == i, turned, line)
        taps_rows[c] = line * scale

    @pl.loop(0, GROUP)
    def _(c):
        before = jnp.zeros((LANES, LANES), F32)
        for k in range(blocks):
            if k < reach:
                line = jnp.broadcast_to(taps_rows[c, pl.ds(k, 1), :], (LANES, LANES))
                turned = pltpu.roll(line, 0, 1, stride=1, stride_axis=0)
            else:
                turned = jnp.zeros((LANES, LANES), F32)
            toeplitz[c, k] = jnp.where(after, turned, before).astype(BF16)
            before = turned

    convolve(0)
    take_in(1)
    convolve(1)
    correlate(1)

    total = terms[...] * scale
    at_col = lax.broadcasted_iota(jnp.int32, total.shape, 2) // depth
    at_line = lax.broadcasted_iota(jnp.int32, total.shape, 1)
    crossed = jnp.zeros_like(total)
    for d in range(GROUP):
        moved = total if d == 0 else pltpu.roll(pltpu.roll(total, GROUP - d, 1), d * depth, 2)
        crossed = jnp.where(lax.rem(at_col - at_line + GROUP, GROUP) == d, moved, crossed)
    term_out[...] = crossed.reshape(peers, LANES)
    place = local_piece * slabs + slab

    @pl.loop(0, peers)
    def _(n):
        @pl.when(jnp.logical_or(jnp.logical_not(at_home), n > 0))
        def _():
            other = lax.rem(me + n, peers)
            copy(
                term_out.at[pl.ds(other, 1)],
                owned.at[pl.ds(place, 1)],
                5,
                {"ctx": other, "ch": mine},
            ).start()

    @pl.when(at_home)
    def _():
        owned[pl.ds(place, 1)] = term_out[pl.ds(me, 1)]

    for part in range(2):
        received(recv_out.at[part], peers - 1, 2 + part)
    lead_half = recv_out[0].astype(F32)
    tail_half = recv_out[1].astype(F32)
    conv = jnp.where(first_half, lead_half, pltpu.roll(tail_half, half, 1))
    back = jnp.where(first_half, pltpu.roll(lead_half, half, 1), tail_half)
    conv = conv.reshape(chans, tok).T
    back = back.reshape(chans, tok).T
    d_two_ref[...] = (conv * grad_out_ref[...].astype(F32)).astype(BF16)
    d_one_ref[...] = (back * values_ref[...].astype(F32)).astype(BF16)
    d_values_ref[...] = (back * x_one_ref[...].astype(F32)).astype(BF16)

    by_home(received, owned, 5)
    full = jnp.sum(owned[...].reshape(share, slabs, LANES), axis=1)
    full = jnp.broadcast_to(full[:, None, :], (share, GROUP, LANES))
    full = full.reshape(share * GROUP, LANES)
    full = jnp.where(own_group, full, 0.0)
    d_filter_ref[...] = lax.dot_general(
        jnp.where(pick, 1.0, 0.0),
        full,
        (((1,), (1,)), ((), ())),
        precision=lax.Precision.HIGHEST,
        preferred_element_type=F32,
    )

    for part in range(2):
        sent(send_in.at[part], peers - 1, part)
        sent(send_out.at[part], peers - 1, 2 + part)
    by_home(sent, gathered, 4)
    by_home(sent, owned, 5)


def flush(*refs):
    count = len(refs) // 2
    sem = refs[-1]
    moves = [
        pltpu.make_async_copy(refs[n], refs[count + n], sem.at[n]) for n in range(count)
    ]
    for move in moves:
        move.start()
    for move in moves:
        move.wait()


def solution(mesh):
    peers = mesh.shape["ctx"]
    slabs = mesh.shape["ch"]

    def local(x_one, x_two, values, grad_out, filter_raw):
        tok, chans = x_one.shape
        depth, owned = filter_raw.shape
        taps = depth * peers
        reach = taps // LANES
        share = peers // slabs
        blocks = reach + 1
        stream = jax.ShapeDtypeStruct((tok, chans), BF16)
        shapes = (stream, stream, stream, jax.ShapeDtypeStruct((depth, owned), F32))
        vmem = pl.BlockSpec(memory_space=pltpu.VMEM)
        hbm = pl.BlockSpec(memory_space=pltpu.HBM)
        x_one, x_two, values, grad_out, filter_raw = (
            pltpu.with_memory_space_constraint(a, pltpu.HBM)
            for a in (x_one, x_two, values, grad_out, filter_raw)
        )
        results = pl.pallas_call(
            functools.partial(kernel, peers, slabs, 1.0 / math.sqrt(taps)),
            out_shape=shapes,
            in_specs=[hbm] * 5,
            out_specs=[vmem] * 4,
            scratch_shapes=[
                pltpu.VMEM((tok, chans), BF16),
                pltpu.VMEM((tok, chans), BF16),
                pltpu.VMEM((tok, chans), BF16),
                pltpu.VMEM((tok, chans), BF16),
                pltpu.VMEM((depth, owned), BF16),
                pltpu.VMEM((2, peers, GROUP, tok), BF16),
                pltpu.VMEM((2, peers, GROUP, tok), BF16),
                pltpu.VMEM((2, peers, GROUP, tok), BF16),
                pltpu.VMEM((2, peers, GROUP, tok), BF16),
                pltpu.VMEM((peers, GROUP, tok), F32),
                pltpu.VMEM((GROUP, peers + reach, tok), F32),
                pltpu.VMEM((GROUP, peers + reach, tok), F32),
                pltpu.VMEM((GROUP, peers, tok), F32),
                pltpu.VMEM((GROUP, peers, tok), F32),
                pltpu.VMEM((share, LANES), F32),
                pltpu.VMEM((peers, LANES), F32),
                pltpu.VMEM((GROUP, reach, LANES), F32),
                pltpu.VMEM((GROUP, blocks, LANES, LANES), BF16),
                pltpu.VMEM((reach, GROUP, LANES), F32),
                pltpu.VMEM((peers, LANES), F32),
                pltpu.VMEM((peers, LANES), F32),
                pltpu.SemaphoreType.DMA((5,)),
                pltpu.SemaphoreType.DMA((6,)),
                pltpu.SemaphoreType.DMA((6,)),
            ],
            compiler_params=pltpu.CompilerParams(
                collective_id=0, has_side_effects=True, vmem_limit_bytes=40 * 1024 * 1024
            ),
        )(x_one, x_two, values, grad_out, filter_raw)
        return pl.pallas_call(
            flush,
            out_shape=shapes,
            in_specs=[vmem] * 4,
            out_specs=[hbm] * 4,
            scratch_shapes=[pltpu.SemaphoreType.DMA((4,))],
            compiler_params=pltpu.CompilerParams(vmem_limit_bytes=8 * 1024 * 1024),
        )(*results)

    placed = P("ctx", "ch")
    return jax.shard_map(
        local,
        mesh=mesh,
        in_specs=(placed,) * 5,
        out_specs=(placed,) * 4,
        check_vma=False,
    )
```

```python
import functools
import math

import jax
import jax.numpy as jnp
from jax import lax
from jax.experimental import pallas as pl
from jax.experimental.pallas import tpu as pltpu
from jax.sharding import PartitionSpec as P

MESH = pl.DeviceIdType.MESH
F32 = jnp.float32
BF16 = jnp.bfloat16
LANES = 128
GROUP = 8


def kernel(
    peers,
    slabs,
    scale,
    x_one_in,
    x_two_in,
    values_in,
    grad_out_in,
    raw_in,
    d_one_ref,
    d_two_ref,
    d_values_ref,
    d_filter_ref,
    x_one_ref,
    x_two_ref,
    values_ref,
    grad_out_ref,
    raw_ref,
    send_in,
    recv_in,
    send_out,
    recv_out,
    spread,
    prod,
    grad,
    conv_full,
    back_full,
    piece,
    gathered,
    taps_rows,
    toeplitz,
    terms,
    term_out,
    owned,
    load_sem,
    send_sem,
    recv_sem,
):
    me = lax.axis_index("ctx")
    slab = lax.axis_index("ch")
    tok = x_one_ref.shape[0]
    chans = x_one_ref.shape[1]
    share = peers // slabs
    reach = taps_rows.shape[1]
    lead = reach
    blocks = reach + 1
    mine = me // share
    local_piece = lax.rem(me, share)
    at_home = mine == slab

    loads = [
        pltpu.make_async_copy(src, dst, load_sem.at[n])
        for n, (src, dst) in enumerate(
            (
                (x_one_in, x_one_ref),
                (values_in, values_ref),
                (grad_out_in, grad_out_ref),
                (x_two_in, x_two_ref),
                (raw_in, raw_ref),
            )
        )
    ]
    for load in loads:
        load.start()

    barrier = pltpu.get_barrier_semaphore()

    def greet(target):
        pl.semaphore_signal(barrier, inc=1, device_id=target, device_id_type=MESH)

    @pl.loop(0, share * (slabs - 1))
    def _(n):
        other = lax.rem(slab + 1 + n // share, slabs)
        greet({"ctx": slab * share + lax.rem(n, share), "ch": other})

    @pl.when(jnp.logical_not(at_home))
    def _():
        @pl.loop(0, peers)
        def _(n):
            greet({"ctx": lax.rem(me + n, peers), "ch": mine})

    @pl.loop(1, peers)
    def _(step):
        greet({"ctx": lax.rem(me + step, peers)})

    def copy(src, dst, at, target):
        return pltpu.make_async_remote_copy(
            src_ref=src,
            dst_ref=dst,
            send_sem=send_sem.at[at],
            recv_sem=recv_sem.at[at],
            device_id=target,
            device_id_type=MESH,
        )

    def received(ref, count, at):
        rest = ref.at[pl.ds(0, count)]
        copy(rest, rest, at, {"ctx": me}).wait_recv()

    def sent(ref, count, at):
        rest = ref.at[pl.ds(0, count)]
        copy(rest, rest, at, {"ctx": me}).wait_send()

    def by_home(act, ref, at):
        pl.when(at_home)(lambda: act(ref, peers - 1, at))
        pl.when(jnp.logical_not(at_home))(lambda: act(ref, peers, at))

    half = GROUP // 2
    first_half = lax.broadcasted_iota(jnp.int32, (peers, GROUP, tok), 1) < half

    def lay(left, right):
        product = (left[...].astype(F32) * right[...].astype(F32)).T
        return product.reshape(peers, GROUP, tok)

    for load in loads:
        load.wait()
    prods = lay(x_one_ref, values_ref)
    grads = lay(grad_out_ref, x_two_ref)
    send_in[0] = jnp.where(first_half, prods, pltpu.roll(grads, half, 1)).astype(BF16)
    send_in[1] = jnp.where(first_half, pltpu.roll(prods, half, 1), grads).astype(BF16)

    raw = raw_ref[...]
    depth = raw.shape[0]
    row = lax.broadcasted_iota(jnp.int32, (depth, LANES), 0)
    col = lax.broadcasted_iota(jnp.int32, (depth, LANES), 1)
    pick = lax.rem(col, depth) == row
    laid = lax.dot_general(
        raw,
        jnp.where(pick, 1.0, 0.0).astype(BF16),
        (((0,), (0,)), ((), ())),
        preferred_element_type=F32,
    )
    at_row = lax.broadcasted_iota(jnp.int32, laid.shape, 0)
    at_col = lax.broadcasted_iota(jnp.int32, laid.shape, 1)
    own_group = lax.rem(at_row, GROUP) == at_col // depth
    laid = jnp.where(own_group, laid, 0.0)
    piece[...] = jnp.sum(laid.reshape(share, GROUP, LANES), axis=1)

    prod[:, pl.ds(0, lead), :] = jnp.zeros((GROUP, lead, LANES), F32)
    grad[:, pl.ds(peers, lead), :] = jnp.zeros((GROUP, lead, LANES), F32)

    pl.semaphore_wait(
        barrier, peers - 1 + share * (slabs - 1) + jnp.where(at_home, 0, peers)
    )

    def exchange(source, target, part, at):
        @pl.loop(1, peers)
        def _(step):
            other = lax.rem(me + step, peers)
            copy(source.at[part, other], target.at[part, me], at + part, {"ctx": other}).start()

    @pl.loop(0, share * slabs)
    def _(n):
        turn, q = n // share, lax.rem(n, share)
        itself = jnp.logical_and(at_home, jnp.logical_and(turn == 0, q == local_piece))

        @pl.when(jnp.logical_not(itself))
        def _():
            copy(
                piece.at[pl.ds(q, 1)],
                gathered.at[pl.ds(me, 1)],
                4,
                {"ctx": slab * share + q, "ch": lax.rem(slab + turn, slabs)},
            ).start()

    exchange(send_in, recv_in, 0, 0)
    exchange(send_in, recv_in, 1, 0)
    for part in range(2):
        recv_in[part, pl.ds(me, 1)] = send_in[part, pl.ds(me, 1)]

    @pl.when(at_home)
    def _():
        gathered[pl.ds(me, 1)] = piece[pl.ds(local_piece, 1)]

    lower = lax.broadcasted_iota(jnp.int32, (LANES, LANES), 0)
    upper = lax.broadcasted_iota(jnp.int32, (LANES, LANES), 1)
    after = upper >= lower
    within = upper <= lower
    flip = jnp.where(upper + lower == LANES - 1, 1.0, 0.0).astype(BF16)

    def take_in(part):
        received(recv_in.at[part], peers - 1, part)
        spread[...] = recv_in[part].astype(F32)
        for c in range(half):
            prod[part * half + c, pl.ds(lead, peers), :] = spread[:, c, :]
            grad[part * half + c, pl.ds(0, peers), :] = spread[:, half + c, :]

    def correlate(part):
        @pl.loop(part * half, part * half + half)
        def _(c):
            wide = jnp.concatenate(
                [grad[c, pl.ds(k, peers), :].astype(BF16) for k in range(blocks)], axis=1
            )
            own = prod[c, pl.ds(lead, peers), :].astype(BF16)
            turned_own = lax.dot_general(
                flip, own, (((1,), (1,)), ((), ())), preferred_element_type=F32
            ).astype(BF16)
            cross = jnp.dot(turned_own, wide, preferred_element_type=F32)
            turned = [
                pltpu.roll(cross[:, k * LANES : (k + 1) * LANES], 1, 1, stride=1, stride_axis=0)
                for k in range(blocks)
            ]
            for k in range(reach):
                both = jnp.where(within, turned[k], turned[k + 1])
                terms[k, pl.ds(c, 1), :] = jnp.sum(both, axis=0, keepdims=True)

    def convolve(part):
        @pl.loop(part * half, part * half + half)
        def _(c):
            wide = jnp.concatenate(
                [prod[c, pl.ds(lead - k, peers), :].astype(BF16) for k in range(blocks)], axis=1
            )
            tall = jnp.concatenate([toeplitz[c, k] for k in range(blocks)], axis=0)
            conv_full[c] = jnp.dot(wide, tall, preferred_element_type=F32)
            wide = jnp.concatenate(
                [grad[c, pl.ds(k, peers), :].astype(BF16) for k in range(blocks)], axis=1
            )
            flat = jnp.concatenate([toeplitz[c, k] for k in range(blocks)], axis=1)
            back_full[c] = lax.dot_general(
                wide, flat, (((1,), (1,)), ((), ())), preferred_element_type=F32
            )

        for c in range(half):
            spread[:, c, :] = conv_full[part * half + c]
            spread[:, half + c, :] = back_full[part * half + c]
        send_out[part] = spread[...].astype(BF16)
        exchange(send_out, recv_out, part, 2)
        recv_out[part, pl.ds(me, 1)] = send_out[part, pl.ds(me, 1)]

    by_home(received, gathered, 4)
    lane_group = lax.broadcasted_iota(jnp.int32, (reach, LANES), 1) // depth
    sources = [gathered[pl.ds(i, reach, stride=GROUP), :] for i in range(GROUP)]
    for c in range(GROUP):
        line = jnp.zeros((reach, LANES), F32)
        for i in range(GROUP):
            turned = pltpu.roll(sources[i], ((i - c) * depth) % LANES, 1)
            line = jnp.where(lane_group == i, turned, line)
        taps_rows[c] = line * scale

    @pl.loop(0, GROUP)
    def _(c):
        before = jnp.zeros((LANES, LANES), F32)
        for k in range(blocks):
            if k < reach:
                line = jnp.broadcast_to(taps_rows[c, pl.ds(k, 1), :], (LANES, LANES))
                turned = pltpu.roll(line, 0, 1, stride=1, stride_axis=0)
            else:
                turned = jnp.zeros((LANES, LANES), F32)
            toeplitz[c, k] = jnp.where(after, turned, before).astype(BF16)
            before = turned

    take_in(0)
    convolve(0)
    correlate(0)
    take_in(1)
    correlate(1)

    total = terms[...] * scale
    at_col = lax.broadcasted_iota(jnp.int32, total.shape, 2) // depth
    at_line = lax.broadcasted_iota(jnp.int32, total.shape, 1)
    crossed = jnp.zeros_like(total)
    for d in range(GROUP):
        moved = total if d == 0 else pltpu.roll(pltpu.roll(total, GROUP - d, 1), d * depth, 2)
        crossed = jnp.where(lax.rem(at_col - at_line + GROUP, GROUP) == d, moved, crossed)
    term_out[...] = crossed.reshape(peers, LANES)
    place = local_piece * slabs + slab

    @pl.loop(0, peers)
    def _(n):
        @pl.when(jnp.logical_or(jnp.logical_not(at_home), n > 0))
        def _():
            other = lax.rem(me + n, peers)
            copy(
                term_out.at[pl.ds(other, 1)],
                owned.at[pl.ds(place, 1)],
                5,
                {"ctx": other, "ch": mine},
            ).start()

    @pl.when(at_home)
    def _():
        owned[pl.ds(place, 1)] = term_out[pl.ds(me, 1)]

    convolve(1)

    for part in range(2):
        received(recv_out.at[part], peers - 1, 2 + part)
    lead_half = recv_out[0].astype(F32)
    tail_half = recv_out[1].astype(F32)
    conv = jnp.where(first_half, lead_half, pltpu.roll(tail_half, half, 1))
    back = jnp.where(first_half, pltpu.roll(lead_half, half, 1), tail_half)
    conv = conv.reshape(chans, tok).T
    back = back.reshape(chans, tok).T
    d_two_ref[...] = (conv * grad_out_ref[...].astype(F32)).astype(BF16)
    d_one_ref[...] = (back * values_ref[...].astype(F32)).astype(BF16)
    d_values_ref[...] = (back * x_one_ref[...].astype(F32)).astype(BF16)

    by_home(received, owned, 5)
    full = jnp.sum(owned[...].reshape(share, slabs, LANES), axis=1)
    full = jnp.broadcast_to(full[:, None, :], (share, GROUP, LANES))
    full = full.reshape(share * GROUP, LANES)
    full = jnp.where(own_group, full, 0.0)
    d_filter_ref[...] = lax.dot_general(
        jnp.where(pick, 1.0, 0.0),
        full,
        (((1,), (1,)), ((), ())),
        precision=lax.Precision.HIGHEST,
        preferred_element_type=F32,
    )

    for part in range(2):
        sent(send_in.at[part], peers - 1, part)
        sent(send_out.at[part], peers - 1, 2 + part)
    by_home(sent, gathered, 4)
    by_home(sent, owned, 5)


def flush(*refs):
    count = len(refs) // 2
    sem = refs[-1]
    moves = [
        pltpu.make_async_copy(refs[n], refs[count + n], sem.at[n]) for n in range(count)
    ]
    for move in moves:
        move.start()
    for move in moves:
        move.wait()


def solution(mesh):
    peers = mesh.shape["ctx"]
    slabs = mesh.shape["ch"]

    def local(x_one, x_two, values, grad_out, filter_raw):
        tok, chans = x_one.shape
        depth, owned = filter_raw.shape
        taps = depth * peers
        reach = taps // LANES
        share = peers // slabs
        blocks = reach + 1
        stream = jax.ShapeDtypeStruct((tok, chans), BF16)
        shapes = (stream, stream, stream, jax.ShapeDtypeStruct((depth, owned), F32))
        vmem = pl.BlockSpec(memory_space=pltpu.VMEM)
        hbm = pl.BlockSpec(memory_space=pltpu.HBM)
        x_one, x_two, values, grad_out, filter_raw = (
            pltpu.with_memory_space_constraint(a, pltpu.HBM)
            for a in (x_one, x_two, values, grad_out, filter_raw)
        )
        results = pl.pallas_call(
            functools.partial(kernel, peers, slabs, 1.0 / math.sqrt(taps)),
            out_shape=shapes,
            in_specs=[hbm] * 5,
            out_specs=[vmem] * 4,
            scratch_shapes=[
                pltpu.VMEM((tok, chans), BF16),
                pltpu.VMEM((tok, chans), BF16),
                pltpu.VMEM((tok, chans), BF16),
                pltpu.VMEM((tok, chans), BF16),
                pltpu.VMEM((depth, owned), BF16),
                pltpu.VMEM((2, peers, GROUP, tok), BF16),
                pltpu.VMEM((2, peers, GROUP, tok), BF16),
                pltpu.VMEM((2, peers, GROUP, tok), BF16),
                pltpu.VMEM((2, peers, GROUP, tok), BF16),
                pltpu.VMEM((peers, GROUP, tok), F32),
                pltpu.VMEM((GROUP, peers + reach, tok), F32),
                pltpu.VMEM((GROUP, peers + reach, tok), F32),
                pltpu.VMEM((GROUP, peers, tok), F32),
                pltpu.VMEM((GROUP, peers, tok), F32),
                pltpu.VMEM((share, LANES), F32),
                pltpu.VMEM((peers, LANES), F32),
                pltpu.VMEM((GROUP, reach, LANES), F32),
                pltpu.VMEM((GROUP, blocks, LANES, LANES), BF16),
                pltpu.VMEM((reach, GROUP, LANES), F32),
                pltpu.VMEM((peers, LANES), F32),
                pltpu.VMEM((peers, LANES), F32),
                pltpu.SemaphoreType.DMA((5,)),
                pltpu.SemaphoreType.DMA((6,)),
                pltpu.SemaphoreType.DMA((6,)),
            ],
            compiler_params=pltpu.CompilerParams(
                collective_id=0, has_side_effects=True, vmem_limit_bytes=40 * 1024 * 1024
            ),
        )(x_one, x_two, values, grad_out, filter_raw)
        return pl.pallas_call(
            flush,
            out_shape=shapes,
            in_specs=[vmem] * 4,
            out_specs=[hbm] * 4,
            scratch_shapes=[pltpu.SemaphoreType.DMA((4,))],
            compiler_params=pltpu.CompilerParams(vmem_limit_bytes=8 * 1024 * 1024),
        )(*results)

    placed = P("ctx", "ch")
    return jax.shard_map(
        local,
        mesh=mesh,
        in_specs=(placed,) * 5,
        out_specs=(placed,) * 4,
        check_vma=False,
    )
```

```python
import functools
import math

import jax
import jax.numpy as jnp
from jax import lax
from jax.experimental import pallas as pl
from jax.experimental.pallas import tpu as pltpu
from jax.sharding import PartitionSpec as P

MESH = pl.DeviceIdType.MESH
F32 = jnp.float32
BF16 = jnp.bfloat16
LANES = 128
GROUP = 8


def kernel(
    peers,
    slabs,
    scale,
    x_one_in,
    x_two_in,
    values_in,
    grad_out_in,
    raw_in,
    d_one_ref,
    d_two_ref,
    d_values_ref,
    d_filter_ref,
    x_one_ref,
    x_two_ref,
    values_ref,
    grad_out_ref,
    raw_ref,
    send_in,
    recv_in,
    send_out,
    recv_out,
    spread,
    prod,
    grad,
    conv_full,
    back_full,
    piece,
    gathered,
    taps_rows,
    toeplitz,
    terms,
    term_out,
    owned,
    load_sem,
    send_sem,
    recv_sem,
):
    me = lax.axis_index("ctx")
    slab = lax.axis_index("ch")
    tok = x_one_ref.shape[0]
    chans = x_one_ref.shape[1]
    share = peers // slabs
    reach = taps_rows.shape[1]
    lead = reach
    blocks = reach + 1
    mine = me // share
    local_piece = lax.rem(me, share)
    at_home = mine == slab

    loads = [
        pltpu.make_async_copy(src, dst, load_sem.at[n])
        for n, (src, dst) in enumerate(
            (
                (x_one_in, x_one_ref),
                (values_in, values_ref),
                (grad_out_in, grad_out_ref),
                (x_two_in, x_two_ref),
                (raw_in, raw_ref),
            )
        )
    ]
    for load in loads:
        load.start()

    barrier = pltpu.get_barrier_semaphore()

    def greet(target):
        pl.semaphore_signal(barrier, inc=1, device_id=target, device_id_type=MESH)

    @pl.when(jnp.logical_not(at_home))
    def _():
        @pl.loop(0, peers, unroll=7)
        def _(n):
            greet({"ctx": lax.rem(me + n, peers), "ch": mine})

    @pl.loop(1, peers, unroll=7)
    def _(step):
        greet({"ctx": lax.rem(me + step, peers)})

    def copy(src, dst, at, target):
        return pltpu.make_async_remote_copy(
            src_ref=src,
            dst_ref=dst,
            send_sem=send_sem.at[at],
            recv_sem=recv_sem.at[at],
            device_id=target,
            device_id_type=MESH,
        )

    def received(ref, count, at):
        rest = ref.at[pl.ds(0, count)]
        copy(rest, rest, at, {"ctx": me}).wait_recv()

    def sent(ref, count, at):
        rest = ref.at[pl.ds(0, count)]
        copy(rest, rest, at, {"ctx": me}).wait_send()

    def by_home(act, ref, at):
        pl.when(at_home)(lambda: act(ref, peers - 1, at))
        pl.when(jnp.logical_not(at_home))(lambda: act(ref, peers, at))

    half = GROUP // 2
    first_half = lax.broadcasted_iota(jnp.int32, (peers, GROUP, tok), 1) < half

    def lay(left, right):
        product = (left[...].astype(F32) * right[...].astype(F32)).T
        return product.reshape(peers, GROUP, tok)

    for load in loads:
        load.wait()
    prods = lay(x_one_ref, values_ref)
    grads = lay(grad_out_ref, x_two_ref)
    send_in[0] = jnp.where(first_half, prods, pltpu.roll(grads, half, 1)).astype(BF16)
    send_in[1] = jnp.where(first_half, pltpu.roll(prods, half, 1), grads).astype(BF16)

    raw = raw_ref[...]
    depth = raw.shape[0]
    row = lax.broadcasted_iota(jnp.int32, (depth, LANES), 0)
    col = lax.broadcasted_iota(jnp.int32, (depth, LANES), 1)
    pick = lax.rem(col, depth) == row
    laid = lax.dot_general(
        raw,
        jnp.where(pick, 1.0, 0.0).astype(BF16),
        (((0,), (0,)), ((), ())),
        preferred_element_type=F32,
    )
    at_row = lax.broadcasted_iota(jnp.int32, laid.shape, 0)
    at_col = lax.broadcasted_iota(jnp.int32, laid.shape, 1)
    own_group = lax.rem(at_row, GROUP) == at_col // depth
    laid = jnp.where(own_group, laid, 0.0)
    piece[...] = jnp.sum(laid.reshape(share, GROUP, LANES), axis=1)

    prod[:, pl.ds(0, lead), :] = jnp.zeros((GROUP, lead, LANES), F32)
    grad[:, pl.ds(peers, lead), :] = jnp.zeros((GROUP, lead, LANES), F32)

    pl.semaphore_wait(barrier, peers - 1 + share * (slabs - 1))

    def exchange(source, target, part, at):
        @pl.loop(1, peers)
        def _(step):
            other = lax.rem(me + step, peers)
            copy(source.at[part, other], target.at[part, me], at + part, {"ctx": other}).start()

    @pl.loop(0, share * slabs)
    def _(n):
        turn, q = n // share, lax.rem(n, share)
        itself = jnp.logical_and(at_home, jnp.logical_and(turn == 0, q == local_piece))

        @pl.when(jnp.logical_not(itself))
        def _():
            copy(
                piece.at[pl.ds(q, 1)],
                gathered.at[pl.ds(me, 1)],
                4,
                {"ctx": slab * share + q, "ch": lax.rem(slab + turn, slabs)},
            ).start()

    exchange(send_in, recv_in, 0, 0)
    exchange(send_in, recv_in, 1, 0)
    for part in range(2):
        recv_in[part, pl.ds(me, 1)] = send_in[part, pl.ds(me, 1)]

    @pl.when(at_home)
    def _():
        gathered[pl.ds(me, 1)] = piece[pl.ds(local_piece, 1)]

    lower = lax.broadcasted_iota(jnp.int32, (LANES, LANES), 0)
    upper = lax.broadcasted_iota(jnp.int32, (LANES, LANES), 1)
    after = upper >= lower
    within = upper <= lower
    flip = jnp.where(upper + lower == LANES - 1, 1.0, 0.0).astype(BF16)

    def take_in(part):
        received(recv_in.at[part], peers - 1, part)
        spread[...] = recv_in[part].astype(F32)
        for c in range(half):
            prod[part * half + c, pl.ds(lead, peers), :] = spread[:, c, :]
            grad[part * half + c, pl.ds(0, peers), :] = spread[:, half + c, :]

    def correlate(part):
        @pl.loop(part * half, part * half + half, unroll=2)
        def _(c):
            wide = jnp.concatenate(
                [grad[c, pl.ds(k, peers), :].astype(BF16) for k in range(blocks)], axis=1
            )
            own = prod[c, pl.ds(lead, peers), :].astype(BF16)
            turned_own = lax.dot_general(
                flip, own, (((1,), (1,)), ((), ())), preferred_element_type=F32
            ).astype(BF16)
            cross = jnp.dot(turned_own, wide, preferred_element_type=F32)
            turned = [
                pltpu.roll(cross[:, k * LANES : (k + 1) * LANES], 1, 1, stride=1, stride_axis=0)
                for k in range(blocks)
            ]
            for k in range(reach):
                both = jnp.where(within, turned[k], turned[k + 1])
                terms[k, pl.ds(c, 1), :] = jnp.sum(both, axis=0, keepdims=True)

    def convolve(part):
        @pl.loop(part * half, part * half + half, unroll=2)
        def _(c):
            wide = jnp.concatenate(
                [prod[c, pl.ds(lead - k, peers), :].astype(BF16) for k in range(blocks)], axis=1
            )
            tall = jnp.concatenate([toeplitz[c, k] for k in range(blocks)], axis=0)
            conv_full[c] = jnp.dot(wide, tall, preferred_element_type=F32)
            wide = jnp.concatenate(
                [grad[c, pl.ds(k, peers), :].astype(BF16) for k in range(blocks)], axis=1
            )
            flat = jnp.concatenate([toeplitz[c, k] for k in range(blocks)], axis=1)
            back_full[c] = lax.dot_general(
                wide, flat, (((1,), (1,)), ((), ())), preferred_element_type=F32
            )

        for c in range(half):
            spread[:, c, :] = conv_full[part * half + c]
            spread[:, half + c, :] = back_full[part * half + c]
        send_out[part] = spread[...].astype(BF16)
        exchange(send_out, recv_out, part, 2)
        recv_out[part, pl.ds(me, 1)] = send_out[part, pl.ds(me, 1)]

    by_home(received, gathered, 4)
    lane_group = lax.broadcasted_iota(jnp.int32, (reach, LANES), 1) // depth
    sources = [gathered[pl.ds(i, reach, stride=GROUP), :] for i in range(GROUP)]
    for c in range(GROUP):
        line = jnp.zeros((reach, LANES), F32)
        for i in range(GROUP):
            turned = pltpu.roll(sources[i], ((i - c) * depth) % LANES, 1)
            line = jnp.where(lane_group == i, turned, line)
        taps_rows[c] = line * scale

    @pl.loop(0, GROUP, unroll=GROUP)
    def _(c):
        before = jnp.zeros((LANES, LANES), F32)
        for k in range(blocks):
            if k < reach:
                line = jnp.broadcast_to(taps_rows[c, pl.ds(k, 1), :], (LANES, LANES))
                turned = pltpu.roll(line, 0, 1, stride=1, stride_axis=0)
            else:
                turned = jnp.zeros((LANES, LANES), F32)
            toeplitz[c, k] = jnp.where(after, turned, before).astype(BF16)
            before = turned

    take_in(0)
    convolve(0)
    correlate(0)
    take_in(1)
    correlate(1)

    total = terms[...] * scale
    at_col = lax.broadcasted_iota(jnp.int32, total.shape, 2) // depth
    at_line = lax.broadcasted_iota(jnp.int32, total.shape, 1)
    crossed = jnp.zeros_like(total)
    for d in range(GROUP):
        moved = total if d == 0 else pltpu.roll(pltpu.roll(total, GROUP - d, 1), d * depth, 2)
        crossed = jnp.where(lax.rem(at_col - at_line + GROUP, GROUP) == d, moved, crossed)
    term_out[...] = crossed.reshape(peers, LANES)
    place = local_piece * slabs + slab

    @pl.loop(0, peers)
    def _(n):
        @pl.when(jnp.logical_or(jnp.logical_not(at_home), n > 0))
        def _():
            other = lax.rem(me + n, peers)
            copy(
                term_out.at[pl.ds(other, 1)],
                owned.at[pl.ds(place, 1)],
                5,
                {"ctx": other, "ch": mine},
            ).start()

    @pl.when(at_home)
    def _():
        owned[pl.ds(place, 1)] = term_out[pl.ds(me, 1)]

    convolve(1)

    for part in range(2):
        received(recv_out.at[part], peers - 1, 2 + part)
    lead_half = recv_out[0].astype(F32)
    tail_half = recv_out[1].astype(F32)
    conv = jnp.where(first_half, lead_half, pltpu.roll(tail_half, half, 1))
    back = jnp.where(first_half, pltpu.roll(lead_half, half, 1), tail_half)
    conv = conv.reshape(chans, tok).T
    back = back.reshape(chans, tok).T
    d_two_ref[...] = (conv * grad_out_ref[...].astype(F32)).astype(BF16)
    d_one_ref[...] = (back * values_ref[...].astype(F32)).astype(BF16)
    d_values_ref[...] = (back * x_one_ref[...].astype(F32)).astype(BF16)

    by_home(received, owned, 5)
    full = jnp.sum(owned[...].reshape(share, slabs, LANES), axis=1)
    full = jnp.broadcast_to(full[:, None, :], (share, GROUP, LANES))
    full = full.reshape(share * GROUP, LANES)
    full = jnp.where(own_group, full, 0.0)
    d_filter_ref[...] = lax.dot_general(
        jnp.where(pick, 1.0, 0.0),
        full,
        (((1,), (1,)), ((), ())),
        precision=lax.Precision.HIGHEST,
        preferred_element_type=F32,
    )

    for part in range(2):
        sent(send_in.at[part], peers - 1, part)
        sent(send_out.at[part], peers - 1, 2 + part)
    by_home(sent, gathered, 4)
    by_home(sent, owned, 5)


def flush(*refs):
    count = len(refs) // 2
    sem = refs[-1]
    moves = [
        pltpu.make_async_copy(refs[n], refs[count + n], sem.at[n]) for n in range(count)
    ]
    for move in moves:
        move.start()
    for move in moves:
        move.wait()


def solution(mesh):
    peers = mesh.shape["ctx"]
    slabs = mesh.shape["ch"]

    def local(x_one, x_two, values, grad_out, filter_raw):
        tok, chans = x_one.shape
        depth, owned = filter_raw.shape
        taps = depth * peers
        reach = taps // LANES
        share = peers // slabs
        blocks = reach + 1
        stream = jax.ShapeDtypeStruct((tok, chans), BF16)
        shapes = (stream, stream, stream, jax.ShapeDtypeStruct((depth, owned), F32))
        vmem = pl.BlockSpec(memory_space=pltpu.VMEM)
        hbm = pl.BlockSpec(memory_space=pltpu.HBM)
        x_one, x_two, values, grad_out, filter_raw = (
            pltpu.with_memory_space_constraint(a, pltpu.HBM)
            for a in (x_one, x_two, values, grad_out, filter_raw)
        )
        results = pl.pallas_call(
            functools.partial(kernel, peers, slabs, 1.0 / math.sqrt(taps)),
            out_shape=shapes,
            in_specs=[hbm] * 5,
            out_specs=[vmem] * 4,
            scratch_shapes=[
                pltpu.VMEM((tok, chans), BF16),
                pltpu.VMEM((tok, chans), BF16),
                pltpu.VMEM((tok, chans), BF16),
                pltpu.VMEM((tok, chans), BF16),
                pltpu.VMEM((depth, owned), BF16),
                pltpu.VMEM((2, peers, GROUP, tok), BF16),
                pltpu.VMEM((2, peers, GROUP, tok), BF16),
                pltpu.VMEM((2, peers, GROUP, tok), BF16),
                pltpu.VMEM((2, peers, GROUP, tok), BF16),
                pltpu.VMEM((peers, GROUP, tok), F32),
                pltpu.VMEM((GROUP, peers + reach, tok), F32),
                pltpu.VMEM((GROUP, peers + reach, tok), F32),
                pltpu.VMEM((GROUP, peers, tok), F32),
                pltpu.VMEM((GROUP, peers, tok), F32),
                pltpu.VMEM((share, LANES), F32),
                pltpu.VMEM((peers, LANES), F32),
                pltpu.VMEM((GROUP, reach, LANES), F32),
                pltpu.VMEM((GROUP, blocks, LANES, LANES), BF16),
                pltpu.VMEM((reach, GROUP, LANES), F32),
                pltpu.VMEM((peers, LANES), F32),
                pltpu.VMEM((peers, LANES), F32),
                pltpu.SemaphoreType.DMA((5,)),
                pltpu.SemaphoreType.DMA((6,)),
                pltpu.SemaphoreType.DMA((6,)),
            ],
            compiler_params=pltpu.CompilerParams(
                collective_id=0, has_side_effects=True, vmem_limit_bytes=40 * 1024 * 1024
            ),
        )(x_one, x_two, values, grad_out, filter_raw)
        return pl.pallas_call(
            flush,
            out_shape=shapes,
            in_specs=[vmem] * 4,
            out_specs=[hbm] * 4,
            scratch_shapes=[pltpu.SemaphoreType.DMA((4,))],
            compiler_params=pltpu.CompilerParams(vmem_limit_bytes=8 * 1024 * 1024),
        )(*results)

    placed = P("ctx", "ch")
    return jax.shard_map(
        local,
        mesh=mesh,
        in_specs=(placed,) * 5,
        out_specs=(placed,) * 4,
        check_vma=False,
    )
```

```python
import functools
import math

import jax
import jax.numpy as jnp
from jax import lax
from jax.experimental import pallas as pl
from jax.experimental.pallas import tpu as pltpu
from jax.sharding import PartitionSpec as P

MESH = pl.DeviceIdType.MESH
F32 = jnp.float32
BF16 = jnp.bfloat16
LANES = 128
GROUP = 8


def kernel(
    peers,
    slabs,
    scale,
    x_one_in,
    x_two_in,
    values_in,
    grad_out_in,
    raw_in,
    d_one_ref,
    d_two_ref,
    d_values_ref,
    d_filter_ref,
    x_one_ref,
    x_two_ref,
    values_ref,
    grad_out_ref,
    raw_ref,
    send_in,
    recv_in,
    send_out,
    recv_out,
    spread,
    prod,
    grad,
    conv_full,
    back_full,
    piece,
    gathered,
    taps_rows,
    toeplitz,
    terms,
    term_out,
    owned,
    load_sem,
    send_sem,
    recv_sem,
):
    me = lax.axis_index("ctx")
    slab = lax.axis_index("ch")
    tok = x_one_ref.shape[0]
    chans = x_one_ref.shape[1]
    share = peers // slabs
    reach = taps_rows.shape[1]
    lead = reach
    blocks = reach + 1
    mine = me // share
    local_piece = lax.rem(me, share)
    at_home = mine == slab

    loads = [
        pltpu.make_async_copy(src, dst, load_sem.at[n])
        for n, (src, dst) in enumerate(
            (
                (x_one_in, x_one_ref),
                (values_in, values_ref),
                (grad_out_in, grad_out_ref),
                (x_two_in, x_two_ref),
                (raw_in, raw_ref),
            )
        )
    ]
    for load in loads:
        load.start()

    barrier = pltpu.get_barrier_semaphore()

    def greet(target):
        pl.semaphore_signal(barrier, inc=1, device_id=target, device_id_type=MESH)

    @pl.when(jnp.logical_not(at_home))
    def _():
        @pl.loop(0, peers, unroll=7)
        def _(n):
            greet({"ctx": lax.rem(me + n, peers), "ch": mine})

    @pl.loop(1, peers, unroll=7)
    def _(step):
        greet({"ctx": lax.rem(me + step, peers)})

    def copy(src, dst, at, target):
        return pltpu.make_async_remote_copy(
            src_ref=src,
            dst_ref=dst,
            send_sem=send_sem.at[at],
            recv_sem=recv_sem.at[at],
            device_id=target,
            device_id_type=MESH,
        )

    def received(ref, count, at):
        rest = ref.at[pl.ds(0, count)]
        copy(rest, rest, at, {"ctx": me}).wait_recv()

    def sent(ref, count, at):
        rest = ref.at[pl.ds(0, count)]
        copy(rest, rest, at, {"ctx": me}).wait_send()

    def by_home(act, ref, at):
        pl.when(at_home)(lambda: act(ref, peers - 1, at))
        pl.when(jnp.logical_not(at_home))(lambda: act(ref, peers, at))

    half = GROUP // 2
    first_half = lax.broadcasted_iota(jnp.int32, (peers, GROUP, tok), 1) < half

    def lay(left, right):
        product = (left[...].astype(F32) * right[...].astype(F32)).T
        return product.reshape(peers, GROUP, tok)

    for load in loads:
        load.wait()
    prods = lay(x_one_ref, values_ref)
    grads = lay(grad_out_ref, x_two_ref)
    send_in[0] = jnp.where(first_half, prods, pltpu.roll(grads, half, 1)).astype(BF16)
    send_in[1] = jnp.where(first_half, pltpu.roll(prods, half, 1), grads).astype(BF16)

    raw = raw_ref[...]
    depth = raw.shape[0]
    row = lax.broadcasted_iota(jnp.int32, (depth, LANES), 0)
    col = lax.broadcasted_iota(jnp.int32, (depth, LANES), 1)
    pick = lax.rem(col, depth) == row
    laid = lax.dot_general(
        raw,
        jnp.where(pick, 1.0, 0.0).astype(BF16),
        (((0,), (0,)), ((), ())),
        preferred_element_type=F32,
    )
    at_row = lax.broadcasted_iota(jnp.int32, laid.shape, 0)
    at_col = lax.broadcasted_iota(jnp.int32, laid.shape, 1)
    own_group = lax.rem(at_row, GROUP) == at_col // depth
    laid = jnp.where(own_group, laid, 0.0)
    piece[...] = jnp.sum(laid.reshape(share, GROUP, LANES), axis=1)

    prod[:, pl.ds(0, lead), :] = jnp.zeros((GROUP, lead, LANES), F32)
    grad[:, pl.ds(peers, lead), :] = jnp.zeros((GROUP, lead, LANES), F32)

    pl.semaphore_wait(barrier, peers - 1 + share * (slabs - 1))

    def exchange(source, target, part, at):
        @pl.loop(1, peers, unroll=7)
        def _(step):
            other = lax.rem(me + step, peers)
            copy(source.at[part, other], target.at[part, me], at + part, {"ctx": other}).start()

    @pl.loop(0, share * slabs, unroll=4)
    def _(n):
        turn, q = n // share, lax.rem(n, share)
        itself = jnp.logical_and(at_home, jnp.logical_and(turn == 0, q == local_piece))

        @pl.when(jnp.logical_not(itself))
        def _():
            copy(
                piece.at[pl.ds(q, 1)],
                gathered.at[pl.ds(me, 1)],
                4,
                {"ctx": slab * share + q, "ch": lax.rem(slab + turn, slabs)},
            ).start()

    exchange(send_in, recv_in, 0, 0)
    exchange(send_in, recv_in, 1, 0)
    for part in range(2):
        recv_in[part, pl.ds(me, 1)] = send_in[part, pl.ds(me, 1)]

    @pl.when(at_home)
    def _():
        gathered[pl.ds(me, 1)] = piece[pl.ds(local_piece, 1)]

    lower = lax.broadcasted_iota(jnp.int32, (LANES, LANES), 0)
    upper = lax.broadcasted_iota(jnp.int32, (LANES, LANES), 1)
    after = upper >= lower
    within = upper <= lower
    flip = jnp.where(upper + lower == LANES - 1, 1.0, 0.0).astype(BF16)

    def take_in(part):
        received(recv_in.at[part], peers - 1, part)
        spread[...] = recv_in[part].astype(F32)
        for c in range(half):
            prod[part * half + c, pl.ds(lead, peers), :] = spread[:, c, :]
            grad[part * half + c, pl.ds(0, peers), :] = spread[:, half + c, :]

    def correlate(part):
        @pl.loop(part * half, part * half + half, unroll=4)
        def _(c):
            wide = jnp.concatenate(
                [grad[c, pl.ds(k, peers), :].astype(BF16) for k in range(blocks)], axis=1
            )
            own = prod[c, pl.ds(lead, peers), :].astype(BF16)
            turned_own = lax.dot_general(
                flip, own, (((1,), (1,)), ((), ())), preferred_element_type=F32
            ).astype(BF16)
            cross = jnp.dot(turned_own, wide, preferred_element_type=F32)
            turned = [
                pltpu.roll(cross[:, k * LANES : (k + 1) * LANES], 1, 1, stride=1, stride_axis=0)
                for k in range(blocks)
            ]
            for k in range(reach):
                both = jnp.where(within, turned[k], turned[k + 1])
                terms[k, pl.ds(c, 1), :] = jnp.sum(both, axis=0, keepdims=True)

    def convolve(part):
        @pl.loop(part * half, part * half + half, unroll=4)
        def _(c):
            wide = jnp.concatenate(
                [prod[c, pl.ds(lead - k, peers), :].astype(BF16) for k in range(blocks)], axis=1
            )
            tall = jnp.concatenate([toeplitz[c, k] for k in range(blocks)], axis=0)
            conv_full[c] = jnp.dot(wide, tall, preferred_element_type=F32)
            wide = jnp.concatenate(
                [grad[c, pl.ds(k, peers), :].astype(BF16) for k in range(blocks)], axis=1
            )
            flat = jnp.concatenate([toeplitz[c, k] for k in range(blocks)], axis=1)
            back_full[c] = lax.dot_general(
                wide, flat, (((1,), (1,)), ((), ())), preferred_element_type=F32
            )

        for c in range(half):
            spread[:, c, :] = conv_full[part * half + c]
            spread[:, half + c, :] = back_full[part * half + c]
        send_out[part] = spread[...].astype(BF16)
        exchange(send_out, recv_out, part, 2)
        recv_out[part, pl.ds(me, 1)] = send_out[part, pl.ds(me, 1)]

    by_home(received, gathered, 4)
    lane_group = lax.broadcasted_iota(jnp.int32, (reach, LANES), 1) // depth
    sources = [gathered[pl.ds(i, reach, stride=GROUP), :] for i in range(GROUP)]
    for c in range(GROUP):
        line = jnp.zeros((reach, LANES), F32)
        for i in range(GROUP):
            turned = pltpu.roll(sources[i], ((i - c) * depth) % LANES, 1)
            line = jnp.where(lane_group == i, turned, line)
        taps_rows[c] = line * scale

    @pl.loop(0, GROUP, unroll=GROUP)
    def _(c):
        before = jnp.zeros((LANES, LANES), F32)
        for k in range(blocks):
            if k < reach:
                line = jnp.broadcast_to(taps_rows[c, pl.ds(k, 1), :], (LANES, LANES))
                turned = pltpu.roll(line, 0, 1, stride=1, stride_axis=0)
            else:
                turned = jnp.zeros((LANES, LANES), F32)
            toeplitz[c, k] = jnp.where(after, turned, before).astype(BF16)
            before = turned

    take_in(0)
    convolve(0)
    correlate(0)
    take_in(1)
    correlate(1)

    total = terms[...] * scale
    at_col = lax.broadcasted_iota(jnp.int32, total.shape, 2) // depth
    at_line = lax.broadcasted_iota(jnp.int32, total.shape, 1)
    crossed = jnp.zeros_like(total)
    for d in range(GROUP):
        moved = total if d == 0 else pltpu.roll(pltpu.roll(total, GROUP - d, 1), d * depth, 2)
        crossed = jnp.where(lax.rem(at_col - at_line + GROUP, GROUP) == d, moved, crossed)
    term_out[...] = crossed.reshape(peers, LANES)
    place = local_piece * slabs + slab

    @pl.loop(0, peers, unroll=4)
    def _(n):
        @pl.when(jnp.logical_or(jnp.logical_not(at_home), n > 0))
        def _():
            other = lax.rem(me + n, peers)
            copy(
                term_out.at[pl.ds(other, 1)],
                owned.at[pl.ds(place, 1)],
                5,
                {"ctx": other, "ch": mine},
            ).start()

    @pl.when(at_home)
    def _():
        owned[pl.ds(place, 1)] = term_out[pl.ds(me, 1)]

    convolve(1)

    for part in range(2):
        received(recv_out.at[part], peers - 1, 2 + part)
    lead_half = recv_out[0].astype(F32)
    tail_half = recv_out[1].astype(F32)
    conv = jnp.where(first_half, lead_half, pltpu.roll(tail_half, half, 1))
    back = jnp.where(first_half, pltpu.roll(lead_half, half, 1), tail_half)
    conv = conv.reshape(chans, tok).T
    back = back.reshape(chans, tok).T
    d_two_ref[...] = (conv * grad_out_ref[...].astype(F32)).astype(BF16)
    d_one_ref[...] = (back * values_ref[...].astype(F32)).astype(BF16)
    d_values_ref[...] = (back * x_one_ref[...].astype(F32)).astype(BF16)

    by_home(received, owned, 5)
    full = jnp.sum(owned[...].reshape(share, slabs, LANES), axis=1)
    full = jnp.broadcast_to(full[:, None, :], (share, GROUP, LANES))
    full = full.reshape(share * GROUP, LANES)
    full = jnp.where(own_group, full, 0.0)
    d_filter_ref[...] = lax.dot_general(
        jnp.where(pick, 1.0, 0.0),
        full,
        (((1,), (1,)), ((), ())),
        precision=lax.Precision.HIGHEST,
        preferred_element_type=F32,
    )

    for part in range(2):
        sent(send_in.at[part], peers - 1, part)
        sent(send_out.at[part], peers - 1, 2 + part)
    by_home(sent, gathered, 4)
    by_home(sent, owned, 5)


def flush(*refs):
    count = len(refs) // 2
    sem = refs[-1]
    moves = [
        pltpu.make_async_copy(refs[n], refs[count + n], sem.at[n]) for n in range(count)
    ]
    for move in moves:
        move.start()
    for move in moves:
        move.wait()


def solution(mesh):
    peers = mesh.shape["ctx"]
    slabs = mesh.shape["ch"]

    def local(x_one, x_two, values, grad_out, filter_raw):
        tok, chans = x_one.shape
        depth, owned = filter_raw.shape
        taps = depth * peers
        reach = taps // LANES
        share = peers // slabs
        blocks = reach + 1
        stream = jax.ShapeDtypeStruct((tok, chans), BF16)
        shapes = (stream, stream, stream, jax.ShapeDtypeStruct((depth, owned), F32))
        vmem = pl.BlockSpec(memory_space=pltpu.VMEM)
        hbm = pl.BlockSpec(memory_space=pltpu.HBM)
        x_one, x_two, values, grad_out, filter_raw = (
            pltpu.with_memory_space_constraint(a, pltpu.HBM)
            for a in (x_one, x_two, values, grad_out, filter_raw)
        )
        results = pl.pallas_call(
            functools.partial(kernel, peers, slabs, 1.0 / math.sqrt(taps)),
            out_shape=shapes,
            in_specs=[hbm] * 5,
            out_specs=[vmem] * 4,
            scratch_shapes=[
                pltpu.VMEM((tok, chans), BF16),
                pltpu.VMEM((tok, chans), BF16),
                pltpu.VMEM((tok, chans), BF16),
                pltpu.VMEM((tok, chans), BF16),
                pltpu.VMEM((depth, owned), BF16),
                pltpu.VMEM((2, peers, GROUP, tok), BF16),
                pltpu.VMEM((2, peers, GROUP, tok), BF16),
                pltpu.VMEM((2, peers, GROUP, tok), BF16),
                pltpu.VMEM((2, peers, GROUP, tok), BF16),
                pltpu.VMEM((peers, GROUP, tok), F32),
                pltpu.VMEM((GROUP, peers + reach, tok), F32),
                pltpu.VMEM((GROUP, peers + reach, tok), F32),
                pltpu.VMEM((GROUP, peers, tok), F32),
                pltpu.VMEM((GROUP, peers, tok), F32),
                pltpu.VMEM((share, LANES), F32),
                pltpu.VMEM((peers, LANES), F32),
                pltpu.VMEM((GROUP, reach, LANES), F32),
                pltpu.VMEM((GROUP, blocks, LANES, LANES), BF16),
                pltpu.VMEM((reach, GROUP, LANES), F32),
                pltpu.VMEM((peers, LANES), F32),
                pltpu.VMEM((peers, LANES), F32),
                pltpu.SemaphoreType.DMA((5,)),
                pltpu.SemaphoreType.DMA((6,)),
                pltpu.SemaphoreType.DMA((6,)),
            ],
            compiler_params=pltpu.CompilerParams(
                collective_id=0, has_side_effects=True, vmem_limit_bytes=40 * 1024 * 1024
            ),
        )(x_one, x_two, values, grad_out, filter_raw)
        return pl.pallas_call(
            flush,
            out_shape=shapes,
            in_specs=[vmem] * 4,
            out_specs=[hbm] * 4,
            scratch_shapes=[pltpu.SemaphoreType.DMA((4,))],
            compiler_params=pltpu.CompilerParams(vmem_limit_bytes=8 * 1024 * 1024),
        )(*results)

    placed = P("ctx", "ch")
    return jax.shard_map(
        local,
        mesh=mesh,
        in_specs=(placed,) * 5,
        out_specs=(placed,) * 4,
        check_vma=False,
    )
```
